512 devices in a mesh: fsdp: 128 (over z, x, core), rep: 4 (over y).
Axes of the slice: x: 4, y: 4, z: 16, core: 2. Of those that a mesh axis runs over, the one named last changes fastest.
Arguments:
- gradients: bfloat16 [4, 512, 48, 3584], P('rep', 'fsdp'), may hold values from -6 to 6
- owner: int32 [336], replicated, may hold values from 0 to 127, as said below
- left_stats: float32 [512, 512, 512], P(('fsdp', 'rep')), may hold values from -0.0625 to 3072, as said below
- right_stats: float32 [512, 512, 512], P(('fsdp', 'rep')), may hold values from -0.0625 to 3072, as said below
Outputs:
- update: bfloat16 [512, 48, 3584], P('fsdp')
The draws below stay inside these ranges and needn't reach their ends.
Inputs may be any that keep to these rules, and one draw needn't show every extreme that they name: No owner holds more than 4 blocks, and some owner holds exactly 4. `left_stats`: each entry is symmetric and positive definite. `right_stats`: each entry is symmetric and positive definite.
All inputs are finite; a program needn't handle non-finite values.
Results may differ from the reference program's by a relative error of at most 0.014.
Values may be sent and summed in bfloat16 or wider, within the bound.
A program may use at most 64 MiB of HBM per device.

```python
import jax
import jax.numpy as jnp
from jax import lax

D = 3584
BS = 512
ITERS = 2
RB = 48
NB = 336
N_FSDP = 128
N_REP = 4


def stats_draw(key, low_diag, high_diag):
    key_diag, key_off = jax.random.split(key)
    entries = N_FSDP * N_REP
    diagonal = jnp.exp(jax.random.uniform(key_diag, (entries, BS), jnp.float32, jnp.log(low_diag), jnp.log(high_diag)))
    spread = 0.5 * low_diag / BS
    noise = jax.random.uniform(key_off, (entries, BS, BS), jnp.float32, -1.0, 1.0) * spread
    symmetric = 0.5 * (noise + jnp.swapaxes(noise, 1, 2))
    identity = jnp.eye(BS, dtype=jnp.float32)
    return symmetric * (1.0 - identity) + identity * diagonal[:, :, None]


def draw_left_stats(key, part):
    key = jax.random.fold_in(key, 11)
    return stats_draw(key, 64.0, 1024.0)


def draw_right_stats(key, part):
    key = jax.random.fold_in(key, 23)
    return stats_draw(key, 64.0, 1024.0)


def draw_owner(key, part):
    key = jax.random.fold_in(key, 5)
    key_rank, key_busy, key_mix = jax.random.split(key, 3)
    total_slots = N_FSDP * N_REP
    priority = jax.random.permutation(key_rank, total_slots)
    busiest = jax.random.randint(key_busy, (), 0, N_FSDP)
    slot_ids = jnp.arange(total_slots, dtype=jnp.int32)
    scores = jnp.where(slot_ids // N_REP == busiest, -1, priority)
    chosen = jnp.argsort(scores, stable=True)[:NB]
    mixed = jax.random.permutation(key_mix, chosen)
    return (mixed // N_REP).astype(jnp.int32)


def levels(key, shape, shards, low, top_value):
    def one(dim, parts):
        heights = jax.random.uniform(jax.random.fold_in(jax.random.fold_in(key, 6), dim), (parts,), jnp.float32, low / len(shards), top_value / len(shards))
        return jnp.repeat(jnp.exp(heights), shape[dim] // parts).reshape((-1,) + (1,) * (len(shape) - dim - 1))

    loudness = one(*shards[0])
    for cut in shards[1:]:
        loudness = loudness * one(*cut)
    return loudness


def gaussian(stream_key, shape, scale, most, pieces=(), kind=jnp.bfloat16):
    result = jax.random.normal(stream_key, shape, jnp.float32) * scale
    if len(pieces) > 0:
        result = levels(stream_key, shape, pieces, -0.22, 0.18) * result
    return jnp.clip(result, min=-most, max=most).astype(kind)


def setup_inputs(seed: int = 0) -> dict:
    key_of = jax.random.split(jax.random.key(seed), 5)
    gradients = gaussian(key_of[0], (N_REP, BS, RB, D), 1.0, 6.0, ((0, 4), (1, 128)))
    owner = draw_owner(jax.random.fold_in(key_of[4], 71), 0)
    left_stats = draw_left_stats(jax.random.fold_in(key_of[4], 71), 0)
    right_stats = draw_right_stats(jax.random.fold_in(key_of[4], 71), 0)
    return {"gradients": gradients, "owner": owner, "left_stats": left_stats, "right_stats": right_stats}


def exact_dot(lhs_mat, rhs_mat):
    return jnp.dot(lhs_mat, rhs_mat, precision=lax.Precision.HIGHEST, preferred_element_type=jnp.float32)

def slot_numbers(owner, owners):
    matches = (owner[:, None] == jnp.arange(owners, dtype=jnp.int32)[None, :]).astype(jnp.int32)
    before = jnp.cumsum(matches, axis=0) - matches
    return lax.optimization_barrier(jnp.sum(before * matches, axis=1)).astype(jnp.int32)

def inverse_fourth_root(matrix):
    extent = matrix.shape[0]
    fro_norm = jnp.sqrt(jnp.sum(matrix * matrix))
    factor = 2.5 / fro_norm
    identity = jnp.eye(extent, dtype=jnp.float32)
    coupled = factor * matrix
    root_mat = identity
    for sweep_index in range(ITERS):
        update_term = (5.0 * identity - coupled) * 0.25
        if sweep_index == 0:
            root_mat = jnp.sqrt(jnp.sqrt(factor)) * update_term
        else:
            root_mat = exact_dot(root_mat, update_term)
        if sweep_index + 1 < ITERS:
            square = exact_dot(update_term, update_term)
            coupled = exact_dot(exact_dot(square, square), coupled)
    return root_mat

def shampoo_block(grad_block, left_stat, right_stat):
    outer_gram = lax.dot_general(grad_block, grad_block, (((1,), (1,)), ((), ())), preferred_element_type=jnp.float32)
    inner_gram = lax.dot_general(grad_block, grad_block, (((0,), (0,)), ((), ())), preferred_element_type=jnp.float32)
    left_root = inverse_fourth_root(left_stat + outer_gram)
    right_root = inverse_fourth_root(right_stat + inner_gram)
    dense_grad = grad_block.astype(jnp.float32)
    shaped = exact_dot(exact_dot(left_root, dense_grad), right_root)
    grad_rms = jnp.sqrt(jnp.mean(dense_grad * dense_grad))
    shaped_rms = jnp.sqrt(jnp.mean(shaped * shaped) + 1e-06)
    return (shaped * (grad_rms / shaped_rms)).astype(jnp.bfloat16)

def reference(gradients, owner, left_stats, right_stats):
    summed = lax.optimization_barrier(jnp.sum(gradients.astype(jnp.float32), axis=0))
    averaged = (summed * (1.0 / N_REP)).astype(jnp.bfloat16)
    slot_of = slot_numbers(owner, N_FSDP)
    grad_blocks = jnp.transpose(averaged.reshape(BS, NB, BS), (1, 0, 2))
    stat_index = (owner * N_REP + slot_of).astype(jnp.int32)
    left_blocks = jnp.take(left_stats, stat_index, axis=0)
    right_blocks = jnp.take(right_stats, stat_index, axis=0)
    updates = lax.map(lambda items: shampoo_block(items[0], items[1], items[2]), (grad_blocks, left_blocks, right_blocks))
    return jnp.transpose(updates, (1, 0, 2)).reshape(BS, RB, D)
```

```python
import functools

import jax
import jax.numpy as jnp
import numpy as np
from jax import lax
from jax.experimental import pallas as pl
from jax.experimental.pallas import tpu as pltpu
from jax.sharding import PartitionSpec as P

MESH = pl.DeviceIdType.MESH
PER_Z = 8
PIECES = 4
ORDER_BITS = 10

F32 = jnp.float32
BF16 = jnp.bfloat16


def mm(lhs, rhs):
    return lax.dot_general(lhs, rhs, (((1,), (0,)), ((), ())), preferred_element_type=F32)


def mm_nt(lhs, rhs):
    return lax.dot_general(lhs, rhs, (((1,), (1,)), ((), ())), preferred_element_type=F32)


def mm_tn(lhs, rhs):
    return lax.dot_general(lhs, rhs, (((0,), (0,)), ((), ())), preferred_element_type=F32)


def one_hot(mask):
    return jnp.where(mask, 1.0, 0.0).astype(BF16)


def newton_root(acc):
    factor = 2.5 / jnp.sqrt(jnp.sum(acc * acc))
    m = acc * factor
    mb = m.astype(BF16)
    q = mm(mb, mb) * 0.0625 - 0.625 * m
    t = 1.5625 * m + mm(q.astype(BF16), mb)
    r = 1.25 * q - 0.25 * t
    rest = -0.3125 * m - 0.25 * (1.953125 * t + mm(r.astype(BF16), t.astype(BF16)))
    return factor, rest


def kernel(
    dims,
    grads,
    rank_row,
    rank_col,
    left,
    right,
    out,
    own,
    stats,
    yrecv,
    zsend,
    zrecv,
    psend,
    precv,
    asend,
    arecv,
    bsend,
    brecv,
    vsend,
    to_key,
    to_block,
    to_slot,
    to_z,
    gmat,
    pmat,
    local_sem,
    send_sem,
    y_sem,
    z_sem,
    p_sem,
    a_sem,
    b_sem,
    out_sem,
    own_sem,
):
    zs, per_z, reps, extent, rb, jb, pieces = dims
    plane = per_z * reps
    width = extent // pieces
    nb = rb * jb
    keys = zs * plane

    f = lax.axis_index("fsdp")
    y = lax.axis_index("rep")
    z = f // per_z
    q = lax.rem(f, per_z)
    p = q * reps + y

    def at_z(other):
        return (other * per_z + q, y)

    def at_p(other):
        return (z * per_z + other // reps, lax.rem(other, reps))

    def at_y(other):
        return (f, other)

    barrier = pltpu.get_barrier_semaphore()

    def greet_z(k, carry):
        pl.semaphore_signal(barrier, inc=1, device_id=at_z(lax.rem(z + k, zs)), device_id_type=MESH)
        return carry

    def greet_p(k, carry):
        pl.semaphore_signal(barrier, inc=1, device_id=at_p(lax.rem(p + k, plane)), device_id_type=MESH)
        return carry

    lax.fori_loop(1, zs, greet_z, 0)
    lax.fori_loop(1, plane, greet_p, 0)

    own_copy = pltpu.make_async_copy(grads.at[y], own, local_sem.at[0])
    own_copy.start()
    left_copy = pltpu.make_async_copy(left.at[0], stats.at[0], local_sem.at[1])
    left_copy.start()
    right_copy = pltpu.make_async_copy(right.at[0], stats.at[1], local_sem.at[2])
    right_copy.start()

    pl.semaphore_wait(barrier, zs - 1 + plane - 1)

    def cols(h, j):
        return pl.ds(j * extent + h * width, width)

    for h in range(pieces):
        def send_y(k, carry):
            other = lax.rem(y + k, reps)
            for j in range(jb):
                pltpu.make_async_remote_copy(
                    src_ref=grads.at[other, :, cols(h, j)],
                    dst_ref=yrecv.at[h, k - 1, j],
                    send_sem=send_sem.at[0],
                    recv_sem=y_sem.at[h],
                    device_id=at_y(other),
                    device_id_type=MESH,
                ).start()
            return carry

        lax.fori_loop(1, reps, send_y, 0)

    rank_r = rank_row[...]
    rank_c = rank_col[...]
    owner_r = rank_r >> ORDER_BITS
    owner_c = rank_c >> ORDER_BITS
    before_r = (rank_c >= (owner_r << ORDER_BITS)) & (rank_c < rank_r)
    slot_r = jnp.sum(jnp.where(before_r, 1.0, 0.0), axis=0, keepdims=True).astype(jnp.int32)
    before_c = (rank_r >= (owner_c << ORDER_BITS)) & (rank_r < rank_c)
    slot_c = jnp.sum(jnp.where(before_c, 1.0, 0.0), axis=1, keepdims=True).astype(jnp.int32)
    key_r = owner_r * reps + slot_r
    key_c = owner_c * reps + slot_c
    to_key[...] = one_hot(lax.broadcasted_iota(jnp.int32, (keys, nb), 0) == key_r)
    to_block[...] = one_hot(lax.broadcasted_iota(jnp.int32, (nb, keys), 1) == key_c)
    row = lax.broadcasted_iota(jnp.int32, (keys, keys), 0)
    col = lax.broadcasted_iota(jnp.int32, (keys, keys), 1)
    z_bits = zs.bit_length() - 1
    p_bits = plane.bit_length() - 1
    to_slot[...] = one_hot(col == ((row & (zs - 1)) << p_bits) + (row >> z_bits))
    to_z[...] = one_hot(col == ((row & (plane - 1)) << z_bits) + (row >> p_bits))

    own_copy.wait()

    def z_far_first(k):
        away = zs // 2 - (k + 1) // 2
        away = jnp.where(lax.rem(k, 2) == 1, away, zs - away)
        return lax.rem(z + away, zs)

    for h in range(pieces):
        pltpu.make_async_copy(yrecv.at[h], yrecv.at[h], y_sem.at[h]).wait()
        parts = []
        for j in range(jb):
            total = own[:, j * extent + h * width : j * extent + (h + 1) * width].astype(F32)
            for k in range(reps - 1):
                total = total + yrecv[h, k, j].astype(F32)
            parts.append((total * (1.0 / reps)).astype(BF16))
        averaged = jnp.concatenate(parts, axis=0)
        zsend[h] = mm(to_key[...], averaged).astype(BF16).reshape(zs, plane, width)

        def send_z(k, carry):
            other = z_far_first(k)
            pltpu.make_async_remote_copy(
                src_ref=zsend.at[h, other],
                dst_ref=zrecv.at[h, z],
                send_sem=send_sem.at[1],
                recv_sem=z_sem.at[h],
                device_id=at_z(other),
                device_id_type=MESH,
            ).start()
            return carry

        lax.fori_loop(0, zs - 1, send_z, 0)
        zrecv[h, z] = zsend[h, z]

    for h in range(pieces):
        pltpu.make_async_copy(
            zrecv.at[h, pl.ds(0, zs - 1)], zrecv.at[h, pl.ds(0, zs - 1)], z_sem.at[h]
        ).wait()
        arrived = zrecv[h].reshape(keys, width)
        psend[h] = mm(to_slot[...], arrived).astype(BF16).reshape(plane, zs, width)

        def send_p(k, carry):
            other = lax.rem(p + k, plane)
            pltpu.make_async_remote_copy(
                src_ref=psend.at[h, other],
                dst_ref=precv.at[h, p],
                send_sem=send_sem.at[2],
                recv_sem=p_sem.at[h],
                device_id=at_p(other),
                device_id_type=MESH,
            ).start()
            return carry

        lax.fori_loop(1, plane, send_p, 0)
        precv[h, p] = psend[h, p]

    for h in range(pieces):
        pltpu.make_async_copy(
            precv.at[h, pl.ds(0, plane - 1)], precv.at[h, pl.ds(0, plane - 1)], p_sem.at[h]
        ).wait()
        arrived = precv[h].reshape(keys, width)
        gmat[:, h * width : (h + 1) * width] = mm(to_z[...], arrived).astype(BF16)

    left_copy.wait()
    right_copy.wait()
    g = gmat[...]
    dense = g.astype(F32)
    left_factor, left_rest = newton_root(stats[0] + mm_nt(g, g))
    right_factor, right_rest = newton_root(stats[1] + mm_tn(g, g))
    half = 1.5625 * dense + mm(left_rest.astype(BF16), g)
    shaped = 1.5625 * half + mm(half.astype(BF16), right_rest.astype(BF16))
    root_scale = jnp.sqrt(jnp.sqrt(left_factor)) * jnp.sqrt(jnp.sqrt(right_factor))
    count = 1.0 / (extent * extent)
    grad_rms = jnp.sqrt(jnp.sum(dense * dense) * count)
    shaped_rms = jnp.sqrt(jnp.sum(shaped * shaped) * count * (root_scale * root_scale) + 1e-06)
    pmat[...] = (shaped * (root_scale * (grad_rms / shaped_rms))).astype(BF16)

    for h in range(pieces):
        rows = pmat[:, h * width : (h + 1) * width]
        asend[h] = mm(to_slot[...], rows).astype(BF16).reshape(plane, zs, width)

        def send_a(k, carry):
            other = lax.rem(p + k, plane)
            pltpu.make_async_remote_copy(
                src_ref=asend.at[h, other],
                dst_ref=arecv.at[h, p],
                send_sem=send_sem.at[3],
                recv_sem=a_sem.at[h],
                device_id=at_p(other),
                device_id_type=MESH,
            ).start()
            return carry

        lax.fori_loop(1, plane, send_a, 0)
        arecv[h, p] = asend[h, p]

    for h in range(pieces):
        pltpu.make_async_copy(
            arecv.at[h, pl.ds(0, plane - 1)], arecv.at[h, pl.ds(0, plane - 1)], a_sem.at[h]
        ).wait()
        arrived = arecv[h].reshape(keys, width)
        bsend[h] = mm(to_z[...], arrived).astype(BF16).reshape(zs, plane, width)

        def send_b(k, carry):
            other = z_far_first(k)
            pltpu.make_async_remote_copy(
                src_ref=bsend.at[h, other],
                dst_ref=brecv.at[h, z],
                send_sem=send_sem.at[4],
                recv_sem=b_sem.at[h],
                device_id=at_z(other),
                device_id_type=MESH,
            ).start()
            return carry

        lax.fori_loop(0, zs - 1, send_b, 0)
        brecv[h, z] = bsend[h, z]

    for h in range(pieces):
        pltpu.make_async_copy(
            brecv.at[h, pl.ds(0, zs - 1)], brecv.at[h, pl.ds(0, zs - 1)], b_sem.at[h]
        ).wait()
        arrived = brecv[h].reshape(keys, width)
        vsend[h] = mm(to_block[...], arrived).astype(BF16).reshape(jb, rb, width)

        def send_out(k, carry):
            other = lax.rem(y + k, reps)
            for j in range(jb):
                pltpu.make_async_remote_copy(
                    src_ref=vsend.at[h, j],
                    dst_ref=out.at[y, :, cols(h, j)],
                    send_sem=send_sem.at[5],
                    recv_sem=out_sem,
                    device_id=at_y(other),
                    device_id_type=MESH,
                ).start()
            return carry

        lax.fori_loop(1, reps, send_out, 0)
        for j in range(jb):
            pltpu.make_async_copy(vsend.at[h, j], out.at[y, :, cols(h, j)], own_sem).start()

    pltpu.make_async_copy(vsend, vsend, own_sem).wait()
    others = pl.ds(0, reps - 1)
    pltpu.make_async_copy(out.at[others], out.at[others], out_sem).wait()
    pltpu.make_async_copy(yrecv, yrecv, send_sem.at[0]).wait()
    pltpu.make_async_copy(out.at[others], out.at[others], send_sem.at[5]).wait()
    for ref, count_, at in (
        (zsend, zs - 1, 1),
        (psend, plane - 1, 2),
        (asend, plane - 1, 3),
        (bsend, zs - 1, 4),
    ):
        sent = ref.at[:, pl.ds(0, count_)]
        pltpu.make_async_copy(sent, sent, send_sem.at[at]).wait()


def per_device(gradients, owner, left_stats, right_stats):
    reps = lax.axis_size("rep")
    owners = lax.axis_size("fsdp")
    rows, rb, width = gradients.shape[1:]
    extent = rows * owners
    jb = width // extent
    nb = rb * jb
    zs = owners // PER_Z
    plane = PER_Z * reps
    w = extent // PIECES
    keys = owners * reps
    assert rows == reps and keys == extent

    number = np.arange(nb, dtype=np.int32).reshape(rb, jb).T.reshape(nb)
    rank = (owner.reshape(rb, jb).T.reshape(nb) << ORDER_BITS) + number
    assert nb <= 1 << ORDER_BITS

    vmem = pl.BlockSpec(memory_space=pltpu.VMEM)
    anywhere = pl.BlockSpec(memory_space=pl.ANY)
    dma = pltpu.SemaphoreType.DMA
    return pl.pallas_call(
        functools.partial(kernel, (zs, PER_Z, reps, extent, rb, jb, PIECES)),
        out_shape=jax.ShapeDtypeStruct((rows, rb, width), BF16),
        in_specs=[anywhere, vmem, vmem, anywhere, anywhere],
        out_specs=anywhere,
        scratch_shapes=[
            pltpu.VMEM((rb, width), BF16),
            pltpu.VMEM((2, extent, extent), F32),
            pltpu.VMEM((PIECES, reps - 1, jb, rb, w), BF16),
            pltpu.VMEM((PIECES, zs, plane, w), BF16),
            pltpu.VMEM((PIECES, zs, plane, w), BF16),
            pltpu.VMEM((PIECES, plane, zs, w), BF16),
            pltpu.VMEM((PIECES, plane, zs, w), BF16),
            pltpu.VMEM((PIECES, plane, zs, w), BF16),
            pltpu.VMEM((PIECES, plane, zs, w), BF16),
            pltpu.VMEM((PIECES, zs, plane, w), BF16),
            pltpu.VMEM((PIECES, zs, plane, w), BF16),
            pltpu.VMEM((PIECES, jb, rb, w), BF16),
            pltpu.VMEM((keys, nb), BF16),
            pltpu.VMEM((nb, keys), BF16),
            pltpu.VMEM((keys, keys), BF16),
            pltpu.VMEM((keys, keys), BF16),
            pltpu.VMEM((extent, extent), BF16),
            pltpu.VMEM((extent, extent), BF16),
            dma((3,)),
            dma((6,)),
            dma((PIECES,)),
            dma((PIECES,)),
            dma((PIECES,)),
            dma((PIECES,)),
            dma((PIECES,)),
            dma,
            dma,
        ],
        compiler_params=pltpu.CompilerParams(
            collective_id=0, has_side_effects=True, vmem_limit_bytes=48 * 1024 * 1024
        ),
    )(gradients[0], rank.reshape(1, nb), rank.reshape(nb, 1), left_stats, right_stats)


def solution(mesh):
    placed = (
        P("rep", "fsdp", None, None),
        P(),
        P(("fsdp", "rep"), None, None),
        P(("fsdp", "rep"), None, None),
    )
    return jax.shard_map(
        per_device, mesh=mesh, in_specs=placed, out_specs=P("fsdp", None, None), check_vma=False
    )
```

```python
import functools

import jax
import jax.numpy as jnp
from jax import lax
from jax.experimental import pallas as pl
from jax.experimental.pallas import tpu as pltpu
from jax.sharding import PartitionSpec as P

MESH = pl.DeviceIdType.MESH
CORES = 2
PER_Z = 8
LANES = 128
MOVES = (
    (2, 2), (1, 2), (3, 2), (2, 1), (2, 3), (1, 1), (3, 3), (1, 3),
    (3, 1), (2, 0), (0, 2), (1, 0), (3, 0), (0, 1), (0, 3), (0, 0),
)

F32 = jnp.float32
BF16 = jnp.bfloat16


def mm(lhs, rhs):
    return lax.dot_general(lhs, rhs, (((1,), (0,)), ((), ())), preferred_element_type=F32)


def mm_nt(lhs, rhs):
    return lax.dot_general(lhs, rhs, (((1,), (1,)), ((), ())), preferred_element_type=F32)


def mm_tn(lhs, rhs):
    return lax.dot_general(lhs, rhs, (((0,), (0,)), ((), ())), preferred_element_type=F32)


def one_hot(mask):
    return jnp.where(mask, 1.0, 0.0).astype(BF16)


def iota(shape, dim):
    return lax.broadcasted_iota(jnp.int32, shape, dim)


def newton_root(acc):
    factor = 2.5 / jnp.sqrt(jnp.sum(acc * acc))
    m = acc * factor
    mb = m.astype(BF16)
    q = mm(mb, mb) * 0.0625 - 0.625 * m
    t = 1.5625 * m + mm(q.astype(BF16), mb)
    r = 1.25 * q - 0.25 * t
    rest = -0.3125 * m - 0.25 * (1.953125 * t + mm(r.astype(BF16), t.astype(BF16)))
    return factor, rest


def wait_bytes(ref, sem):
    pltpu.make_async_copy(ref, ref, sem).wait()


def kernel(dims, owner, grads, left, right, out, s):
    zs, reps, extent, rb, jb, groups, lanes = dims
    xs = PER_Z // CORES
    plane = PER_Z * reps
    nb = rb * jb
    keys = zs * plane

    f = lax.axis_index("fsdp")
    y = lax.axis_index("rep")
    z = f // PER_Z
    q = lax.rem(f, PER_Z)
    x, c = q // CORES, lax.rem(q, CORES)
    p = q * reps + y

    barrier = pltpu.get_barrier_semaphore()

    def greet_z(k, carry):
        to = (lax.rem(z + k, zs) * PER_Z + q, y)
        pl.semaphore_signal(barrier, inc=1, device_id=to, device_id_type=MESH)
        return carry

    def greet_p(k, carry):
        other = lax.rem(p + k, plane)
        to = (z * PER_Z + other // reps, lax.rem(other, reps))
        pl.semaphore_signal(barrier, inc=1, device_id=to, device_id_type=MESH)
        return carry

    rows_copy = pltpu.make_async_copy(grads, s["rows"], s["local_sem"].at[0])
    rows_copy.start()
    lax.fori_loop(1, zs, greet_z, 0)
    lax.fori_loop(1, plane, greet_p, 0)
    left_copy = pltpu.make_async_copy(left.at[0], s["stats"].at[0], s["local_sem"].at[1])
    left_copy.start()
    right_copy = pltpu.make_async_copy(right.at[0], s["stats"].at[1], s["local_sem"].at[2])
    right_copy.start()

    def number(at):
        j = sum(jnp.where(at >= rb * t, 1, 0) for t in range(1, jb))
        return (at - j * rb) * jb + j

    z_bits = zs.bit_length() - 1
    p_bits = plane.bit_length() - 1

    def place(key):
        return ((key & (plane - 1)) << z_bits) + (key >> p_bits)

    blocks = (nb, nb)
    b0, b1 = iota(blocks, 0), iota(blocks, 1)
    owner_r = owner[...].reshape(1, nb)
    owner_c = jnp.sum(jnp.where(b0 == b1, owner_r, 0).astype(F32), axis=1, keepdims=True).astype(jnp.int32)
    same = owner_c == owner_r
    slot_r = jnp.sum(jnp.where(same & (b0 < b1), 1.0, 0.0), axis=0, keepdims=True).astype(jnp.int32)
    key_of = one_hot(iota((keys, nb), 0) == place(owner_r * reps + slot_r))
    s["to_key"][...] = mm(key_of, one_hot(b0 == number(b1))).astype(BF16)

    def gather(h):
        for a in range(reps):
            parts = [s["rows"][a, :, j * extent + h * lanes : j * extent + (h + 1) * lanes] for j in range(jb)]
            picked = mm(s["to_key"][...], jnp.concatenate(parts, axis=0))
            s["ysend"][h, :, a] = picked.astype(BF16).reshape(plane, zs, lanes)

    def plane_sends(source, dest, stage, h):
        def send(core, move):
            qx = lax.rem(x + move[0], xs) * CORES + lax.rem(c + core, CORES)
            py = lax.rem(y + move[1], reps)
            pltpu.make_async_remote_copy(
                src_ref=source(qx, py),
                dst_ref=dest.at[h, p],
                send_sem=s["send_sem"].at[stage],
                recv_sem=s["recv_sem"].at[stage, h],
                device_id=(z * PER_Z + qx, py),
                device_id_type=MESH,
            ).start()

        def step(core, carry):
            for move in MOVES:
                if move != (0, 0):
                    send(core, move)
                else:
                    pl.when(core > 0)(functools.partial(send, core, move))
            return carry

        lax.fori_loop(0, CORES, step, 0)

    def z_send(source, dest, stage, h, other):
        pltpu.make_async_remote_copy(
            src_ref=source.at[h, other],
            dst_ref=dest.at[h, z],
            send_sem=s["send_sem"].at[stage],
            recv_sem=s["recv_sem"].at[stage, h],
            device_id=(other * PER_Z + q, y),
            device_id_type=MESH,
        ).start()

    others_z = pl.ds(0, zs - 1)
    others_p = pl.ds(0, plane - 1)

    rows_copy.wait()
    gather(0)
    pl.semaphore_wait(barrier, zs - 1 + plane - 1)
    for h in range(groups):
        if h > 0:
            gather(h)
        plane_sends(lambda qx, py: s["ysend"].at[h, qx * reps + py], s["yrecv"], 0, h)
        s["yrecv"][h, p] = s["ysend"][h, p]

    row, col = iota((keys, keys), 0), iota((keys, keys), 1)
    s["to_z"][...] = one_hot(col == ((row & (plane - 1)) << z_bits) + (row >> p_bits))

    for h in range(groups):
        wait_bytes(s["yrecv"].at[h, others_p], s["recv_sem"].at[0, h])
        parts = []
        for k in range(PER_Z):
            total = s["yrecv"][h, k * reps].astype(F32)
            for other in range(1, reps):
                total = total + s["yrecv"][h, k * reps + other].astype(F32)
            parts.append((total * (1.0 / reps)).astype(BF16).reshape(reps * zs, lanes))
        averaged = jnp.concatenate(parts, axis=0)
        s["zsend"][h] = mm(s["to_z"][...], averaged).astype(BF16).reshape(zs, plane, lanes)

        def step(k, carry):
            away = zs // 2 - (k + 1) // 2
            odd = lax.rem(k, 2)
            z_send(s["zsend"], s["zrecv"], 1, h, lax.rem(z + odd * away + (1 - odd) * (zs - away), zs))
            return carry

        lax.fori_loop(0, zs - 1, step, 0)
        s["zrecv"][h, z] = s["zsend"][h, z]

    slot_c = jnp.sum(jnp.where(same & (b1 < b0), 1.0, 0.0), axis=1, keepdims=True).astype(jnp.int32)
    of_key = one_hot(iota((nb, keys), 1) == place(owner_c * reps + slot_c))
    s["to_block"][...] = mm(one_hot(b1 == number(b0)), of_key).astype(BF16)
    s["to_slot"][...] = one_hot(col == ((row & (zs - 1)) << p_bits) + (row >> z_bits))

    left_copy.wait()
    right_copy.wait()
    for h in range(groups):
        wait_bytes(s["zrecv"].at[h, others_z], s["recv_sem"].at[1, h])
        s["gmat"][:, h * lanes : (h + 1) * lanes] = s["zrecv"][h].reshape(keys, lanes)
    g = s["gmat"][...]
    dense = g.astype(F32)
    left_factor, left_rest = newton_root(s["stats"][0] + mm_nt(g, g))
    right_factor, right_rest = newton_root(s["stats"][1] + mm_tn(g, g))
    half = 1.5625 * dense + mm(left_rest.astype(BF16), g)
    shaped = 1.5625 * half + mm(half.astype(BF16), right_rest.astype(BF16))
    root_scale = jnp.sqrt(jnp.sqrt(left_factor)) * jnp.sqrt(jnp.sqrt(right_factor))
    mean = 1.0 / (extent * extent)
    grad_rms = jnp.sqrt(jnp.sum(dense * dense) * mean)
    shaped_rms = jnp.sqrt(jnp.sum(shaped * shaped) * mean * (root_scale * root_scale) + 1e-06)
    update = (shaped * (root_scale * (grad_rms / shaped_rms))).astype(BF16)
    for h in range(groups):
        s["bsend"][h] = update[:, h * lanes : (h + 1) * lanes].reshape(zs, plane, lanes)

    for h in range(groups):

        def step(k, carry):
            other = lax.rem(k, 2) * (zs // 2) + k // 2
            pl.when(other != z)(functools.partial(z_send, s["bsend"], s["brecv"], 2, h, other))
            return carry

        lax.fori_loop(0, zs, step, 0)
        s["brecv"][h, z] = s["bsend"][h, z]

    def back(h):
        wait_bytes(s["brecv"].at[h, others_z], s["recv_sem"].at[2, h])
        rows = mm(s["to_slot"][...], s["brecv"][h].reshape(keys, lanes)).astype(BF16)
        s["psend"][h] = rows.reshape(PER_Z, reps, zs, lanes)
        plane_sends(lambda qx, py: s["psend"].at[h, qx], s["precv"], 3, h)
        s["precv"][h, p] = s["psend"][h, q]

    def write(h):
        wait_bytes(s["precv"].at[h, others_p], s["recv_sem"].at[3, h])
        for a in range(reps):
            rows = mm(s["to_block"][...], s["precv"][h, :, a].reshape(keys, lanes)).astype(BF16)
            for j in range(jb):
                at = j * extent + h * lanes
                s["rows"][a, :, at : at + lanes] = rows[j * rb : (j + 1) * rb]
        for j in range(jb):
            at = pl.ds(j * extent + h * lanes, lanes)
            pltpu.make_async_copy(s["rows"].at[:, :, at], out.at[:, :, at], s["local_sem"].at[3]).start()

    for h in range(groups):
        back(h)
        if h > 0:
            write(h - 1)
    write(groups - 1)

    wait_bytes(s["rows"], s["local_sem"].at[3])
    wait_bytes(s["ysend"].at[:, others_p], s["send_sem"].at[0])
    wait_bytes(s["zsend"].at[:, others_z], s["send_sem"].at[1])
    wait_bytes(s["bsend"].at[:, others_z], s["send_sem"].at[2])
    wait_bytes(s["precv"].at[:, others_p], s["send_sem"].at[3])


def per_device(gradients, owner, left_stats, right_stats):
    reps = lax.axis_size("rep")
    owners = lax.axis_size("fsdp")
    rows, rb, width = gradients.shape[1:]
    extent = rows * owners
    jb = width // extent
    nb = rb * jb
    zs = owners // PER_Z
    plane = PER_Z * reps
    groups = extent // LANES
    keys = owners * reps
    assert rows == reps and keys == extent

    vmem = pl.BlockSpec(memory_space=pltpu.VMEM)
    hbm = pl.BlockSpec(memory_space=pltpu.HBM)
    dma = pltpu.SemaphoreType.DMA
    by_z = pltpu.VMEM((groups, zs, plane, LANES), BF16)
    by_place = pltpu.VMEM((groups, plane, rows, zs, LANES), BF16)
    scratch = dict(
        rows=pltpu.VMEM((rows, rb, width), BF16),
        stats=pltpu.VMEM((2, extent, extent), F32),
        ysend=by_place,
        yrecv=by_place,
        zsend=by_z,
        zrecv=by_z,
        bsend=by_z,
        brecv=by_z,
        psend=pltpu.VMEM((groups, PER_Z, rows, zs, LANES), BF16),
        precv=by_place,
        to_key=pltpu.VMEM((keys, nb), BF16),
        to_block=pltpu.VMEM((nb, keys), BF16),
        to_slot=pltpu.VMEM((keys, keys), BF16),
        to_z=pltpu.VMEM((keys, keys), BF16),
        gmat=pltpu.VMEM((extent, extent), BF16),
        local_sem=dma((4,)),
        send_sem=dma((4,)),
        recv_sem=dma((4, groups)),
    )
    return pl.pallas_call(
        functools.partial(kernel, (zs, reps, extent, rb, jb, groups, LANES)),
        out_shape=jax.ShapeDtypeStruct((rows, rb, width), BF16),
        in_specs=[vmem, hbm, hbm, hbm],
        out_specs=pl.BlockSpec(memory_space=pl.ANY),
        scratch_shapes=[scratch],
        compiler_params=pltpu.CompilerParams(
            collective_id=0, has_side_effects=True, vmem_limit_bytes=60 * 1024 * 1024
        ),
    )(owner, gradients[0], left_stats, right_stats)


def solution(mesh):
    placed = (
        P("rep", "fsdp", None, None),
        P(),
        P(("fsdp", "rep"), None, None),
        P(("fsdp", "rep"), None, None),
    )
    return jax.shard_map(
        per_device, mesh=mesh, in_specs=placed, out_specs=P("fsdp", None, None), check_vma=False
    )
```

```python
import functools

import jax
import jax.numpy as jnp
from jax import lax
from jax.experimental import pallas as pl
from jax.experimental.pallas import tpu as pltpu
from jax.sharding import PartitionSpec as P

MESH = pl.DeviceIdType.MESH
CORES = 2
PER_Z = 8
LANES = 128
MOVES = (
    (2, 2), (1, 2), (3, 2), (2, 1), (2, 3), (1, 1), (3, 3), (1, 3),
    (3, 1), (2, 0), (0, 2), (1, 0), (3, 0), (0, 1), (0, 3), (0, 0),
)

F32 = jnp.float32
BF16 = jnp.bfloat16


def mm(lhs, rhs):
    return lax.dot_general(lhs, rhs, (((1,), (0,)), ((), ())), preferred_element_type=F32)


def mm_nt(lhs, rhs):
    return lax.dot_general(lhs, rhs, (((1,), (1,)), ((), ())), preferred_element_type=F32)


def mm_tn(lhs, rhs):
    return lax.dot_general(lhs, rhs, (((0,), (0,)), ((), ())), preferred_element_type=F32)


def one_hot(mask):
    return jnp.where(mask, 1.0, 0.0).astype(BF16)


def iota(shape, dim):
    return lax.broadcasted_iota(jnp.int32, shape, dim)


def newton_root(acc):
    factor = 2.5 / jnp.sqrt(jnp.sum(acc * acc))
    m = acc * factor
    mb = m.astype(BF16)
    q = mm(mb, mb) * 0.0625 - 0.625 * m
    t = 1.5625 * m + mm(q.astype(BF16), mb)
    r = 1.25 * q - 0.25 * t
    rest = -0.3125 * m - 0.25 * (1.953125 * t + mm(r.astype(BF16), t.astype(BF16)))
    return factor, rest


def wait_bytes(ref, sem):
    pltpu.make_async_copy(ref, ref, sem).wait()


def kernel(dims, owner, grads, left, right, out, s):
    zs, reps, extent, rb, jb, groups, lanes = dims
    xs = PER_Z // CORES
    plane = PER_Z * reps
    nb = rb * jb
    keys = zs * plane

    f = lax.axis_index("fsdp")
    y = lax.axis_index("rep")
    z = f // PER_Z
    q = lax.rem(f, PER_Z)
    x, c = q // CORES, lax.rem(q, CORES)
    p = q * reps + y

    barrier = pltpu.get_barrier_semaphore()

    def greet_z(k, carry):
        to = (lax.rem(z + k, zs) * PER_Z + q, y)
        pl.semaphore_signal(barrier, inc=1, device_id=to, device_id_type=MESH)
        return carry

    def greet_p(k, carry):
        other = lax.rem(p + k, plane)
        to = (z * PER_Z + other // reps, lax.rem(other, reps))
        pl.semaphore_signal(barrier, inc=1, device_id=to, device_id_type=MESH)
        return carry

    rows_copy = pltpu.make_async_copy(grads, s["rows"], s["local_sem"].at[0])
    rows_copy.start()
    lax.fori_loop(1, zs, greet_z, 0)
    lax.fori_loop(1, plane, greet_p, 0)
    left_copy = pltpu.make_async_copy(left.at[0], s["stats"].at[0], s["local_sem"].at[1])
    left_copy.start()
    right_copy = pltpu.make_async_copy(right.at[0], s["stats"].at[1], s["local_sem"].at[2])
    right_copy.start()

    near = zs // 2

    def rank(away):
        return jnp.where(away < near, zs - 1 - 2 * away, 2 * (away - near))

    def number(at):
        j = sum(jnp.where(at >= rb * t, 1, 0) for t in range(1, jb))
        return (at - j * rb) * jb + j

    p_bits = plane.bit_length() - 1
    n_bits = near.bit_length() - 1
    part = plane * near

    def place(key):
        r = rank(((key >> p_bits) - z) & (zs - 1))
        return (r >> n_bits) * part + ((key & (plane - 1)) << n_bits) + (r & (near - 1))

    blocks = (nb, nb)
    b0, b1 = iota(blocks, 0), iota(blocks, 1)
    owner_r = owner[...].reshape(1, nb)
    owner_c = jnp.sum(jnp.where(b0 == b1, owner_r, 0).astype(F32), axis=1, keepdims=True).astype(jnp.int32)
    same = owner_c == owner_r
    slot_r = jnp.sum(jnp.where(same & (b0 < b1), 1.0, 0.0), axis=0, keepdims=True).astype(jnp.int32)
    key_of = one_hot(iota((keys, nb), 0) == place(owner_r * reps + slot_r))
    s["to_key"][...] = mm(key_of, one_hot(b0 == number(b1))).astype(BF16)

    def gather(h, half):
        key_rows = s["to_key"][half * part : (half + 1) * part]
        picked = []
        for a in range(reps):
            parts = [s["rows"][a, :, j * extent + h * lanes : j * extent + (h + 1) * lanes] for j in range(jb)]
            picked.append(mm(key_rows, jnp.concatenate(parts, axis=0)).reshape(plane, near, lanes))
        s["ysend"][h, half] = jnp.concatenate(picked, axis=1).astype(BF16)

    def plane_sends(source, dest, stage, h, half):
        def send(core, move):
            qx = lax.rem(x + move[0], xs) * CORES + lax.rem(c + core, CORES)
            py = lax.rem(y + move[1], reps)
            pltpu.make_async_remote_copy(
                src_ref=source(qx, py),
                dst_ref=dest.at[h, half, p],
                send_sem=s["send_sem"].at[stage],
                recv_sem=s["recv_sem"].at[stage, h, half],
                device_id=(z * PER_Z + qx, py),
                device_id_type=MESH,
            ).start()

        def step(core, carry):
            for move in MOVES:
                if move != (0, 0):
                    send(core, move)
                else:
                    pl.when(core > 0)(functools.partial(send, core, move))
            return carry

        lax.fori_loop(0, CORES, step, 0)

    def z_send(source, dest, stage, sem, other):
        pltpu.make_async_remote_copy(
            src_ref=source,
            dst_ref=dest,
            send_sem=s["send_sem"].at[stage],
            recv_sem=sem,
            device_id=(other * PER_Z + q, y),
            device_id_type=MESH,
        ).start()

    others_z = pl.ds(0, zs - 1)
    others_p = pl.ds(0, plane - 1)

    def to_place(h, half):
        plane_sends(lambda qx, py: s["ysend"].at[h, half, qx * reps + py], s["yrecv"], 0, h, half)
        s["yrecv"][h, half, p] = s["ysend"][h, half, p]

    def to_owner(h, half):
        wait_bytes(s["yrecv"].at[h, half, others_p], s["recv_sem"].at[0, h, half])
        parts = []
        for k in range(PER_Z):
            total = s["yrecv"][h, half, k * reps].astype(F32)
            for other in range(1, reps):
                total = total + s["yrecv"][h, half, k * reps + other].astype(F32)
            parts.append((total * (1.0 / reps)).astype(BF16))
        averaged = jnp.concatenate(parts, axis=0)
        s["zsend"][h, half] = mm(s["to_z"][...], averaged).astype(BF16).reshape(near, plane, lanes)

        def step(k, carry):
            r = half * near + k
            odd = lax.rem(r, 2)
            away = near - (r + 1) // 2
            other = lax.rem(z + odd * away + (1 - odd) * (zs - away), zs)
            z_send(s["zsend"].at[h, half, k], s["zrecv"].at[h, z], 1, s["recv_sem"].at[1, h, 0], other)
            return carry

        lax.fori_loop(0, near - half, step, 0)
        if half == 1:
            s["zrecv"][h, z] = s["zsend"][h, 1, near - 1]

    rows_copy.wait()
    gather(0, 0)
    pl.semaphore_wait(barrier, zs - 1 + plane - 1)
    to_place(0, 0)
    row, col = iota((part, part), 0), iota((part, part), 1)
    s["to_z"][...] = one_hot(col == ((row & (plane - 1)) << n_bits) + (row >> p_bits))
    for h in range(1, groups):
        gather(h, 0)
        to_place(h, 0)
    for h in range(groups):
        gather(h, 1)
        to_owner(h, 0)
        to_place(h, 1)
    for h in range(groups):
        to_owner(h, 1)

    slot_c = jnp.sum(jnp.where(same & (b1 < b0), 1.0, 0.0), axis=1, keepdims=True).astype(jnp.int32)
    of_key = one_hot(iota((nb, keys), 1) == place(owner_c * reps + slot_c))
    s["to_block"][...] = mm(one_hot(b1 == number(b0)), of_key).astype(BF16)
    s["to_place"][...] = one_hot(col == ((row & (near - 1)) << p_bits) + (row >> n_bits))

    left_copy.wait()
    right_copy.wait()
    for h in range(groups):
        wait_bytes(s["zrecv"].at[h, others_z], s["recv_sem"].at[1, h, 0])
        s["gmat"][:, h * lanes : (h + 1) * lanes] = s["zrecv"][h].reshape(keys, lanes)
    g = s["gmat"][...]
    dense = g.astype(F32)
    left_factor, left_rest = newton_root(s["stats"][0] + mm_nt(g, g))
    right_factor, right_rest = newton_root(s["stats"][1] + mm_tn(g, g))
    half = 1.5625 * dense + mm(left_rest.astype(BF16), g)
    shaped = 1.5625 * half + mm(half.astype(BF16), right_rest.astype(BF16))
    root_scale = jnp.sqrt(jnp.sqrt(left_factor)) * jnp.sqrt(jnp.sqrt(right_factor))
    mean = 1.0 / (extent * extent)
    grad_rms = jnp.sqrt(jnp.sum(dense * dense) * mean)
    shaped_rms = jnp.sqrt(jnp.sum(shaped * shaped) * mean * (root_scale * root_scale) + 1e-06)
    update = (shaped * (root_scale * (grad_rms / shaped_rms))).astype(BF16)
    for h in range(groups):
        s["bsend"][h] = update[:, h * lanes : (h + 1) * lanes].reshape(zs, plane, lanes)

    def back_z(h, half):
        def send(other, r):
            z_send(s["bsend"].at[h, other], s["brecv"].at[h, half, r], 2, s["recv_sem"].at[2, h, half], other)

        def near_step(k, carry):
            r = zs - 2 - k
            odd = lax.rem(r, 2)
            away = near - (r + 1) // 2
            send(lax.rem(z + odd * (zs - away) + (1 - odd) * away, zs), r - near)
            return carry

        def far_step(k, carry):
            other = lax.rem(k, 2) * near + k // 2
            r = rank(lax.rem(z - other + zs, zs))
            pl.when(r < near)(functools.partial(send, other, r))
            return carry

        if half == 1:
            lax.fori_loop(0, near - 1, near_step, 0)
            s["brecv"][h, 1, near - 1] = s["bsend"][h, z]
        else:
            lax.fori_loop(0, zs, far_step, 0)

    for half in (1, 0):
        for h in range(groups):
            back_z(h, half)

    def back(h, half):
        wait_bytes(s["brecv"].at[h, half, pl.ds(0, near - half)], s["recv_sem"].at[2, h, half])
        rows = mm(s["to_place"][...], s["brecv"][h, half].reshape(part, lanes)).astype(BF16)
        s["psend"][h, half] = rows.reshape(PER_Z, reps * near, lanes)
        plane_sends(lambda qx, py: s["psend"].at[h, half, qx], s["precv"], 3, h, half)
        s["precv"][h, half, p] = s["psend"][h, half, q]

    def write(h):
        pieces = []
        for half in range(2):
            wait_bytes(s["precv"].at[h, half, others_p], s["recv_sem"].at[3, h, half])
            pieces.append(s["precv"][h, half].astype(F32))
        for a in range(reps):
            at_a = [piece[:, a * near : (a + 1) * near].reshape(part, lanes) for piece in pieces]
            rows = mm(s["to_block"][...], jnp.concatenate(at_a, axis=0).astype(BF16)).astype(BF16)
            for j in range(jb):
                at = j * extent + h * lanes
                s["rows"][a, :, at : at + lanes] = rows[j * rb : (j + 1) * rb]
        for j in range(jb):
            at = pl.ds(j * extent + h * lanes, lanes)
            pltpu.make_async_copy(s["rows"].at[:, :, at], out.at[:, :, at], s["local_sem"].at[3]).start()

    for h in range(groups):
        back(h, 1)
    for h in range(groups):
        back(h, 0)
        if h > 0:
            write(h - 1)
    write(groups - 1)

    wait_bytes(s["rows"], s["local_sem"].at[3])
    wait_bytes(s["ysend"].at[:, :, others_p], s["send_sem"].at[0])
    wait_bytes(s["zrecv"].at[:, others_z], s["send_sem"].at[1])
    wait_bytes(s["bsend"].at[:, others_z], s["send_sem"].at[2])
    wait_bytes(s["precv"].at[:, :, others_p], s["send_sem"].at[3])


def per_device(gradients, owner, left_stats, right_stats):
    reps = lax.axis_size("rep")
    owners = lax.axis_size("fsdp")
    rows, rb, width = gradients.shape[1:]
    extent = rows * owners
    jb = width // extent
    nb = rb * jb
    zs = owners // PER_Z
    plane = PER_Z * reps
    groups = extent // LANES
    keys = owners * reps
    assert rows == reps and keys == extent

    vmem = pl.BlockSpec(memory_space=pltpu.VMEM)
    hbm = pl.BlockSpec(memory_space=pltpu.HBM)
    dma = pltpu.SemaphoreType.DMA
    by_z = pltpu.VMEM((groups, zs, plane, LANES), BF16)
    by_half = pltpu.VMEM((groups, 2, zs // 2, plane, LANES), BF16)
    by_place = pltpu.VMEM((groups, 2, plane, rows * zs // 2, LANES), BF16)
    scratch = dict(
        rows=pltpu.VMEM((rows, rb, width), BF16),
        stats=pltpu.VMEM((2, extent, extent), F32),
        ysend=by_place,
        yrecv=by_place,
        zsend=by_half,
        zrecv=by_z,
        bsend=by_z,
        brecv=by_half,
        psend=pltpu.VMEM((groups, 2, PER_Z, rows * zs // 2, LANES), BF16),
        precv=by_place,
        to_key=pltpu.VMEM((keys, nb), BF16),
        to_block=pltpu.VMEM((nb, keys), BF16),
        to_place=pltpu.VMEM((keys // 2, keys // 2), BF16),
        to_z=pltpu.VMEM((keys // 2, keys // 2), BF16),
        gmat=pltpu.VMEM((extent, extent), BF16),
        local_sem=dma((4,)),
        send_sem=dma((4,)),
        recv_sem=dma((4, groups, 2)),
    )
    return pl.pallas_call(
        functools.partial(kernel, (zs, reps, extent, rb, jb, groups, LANES)),
        out_shape=jax.ShapeDtypeStruct((rows, rb, width), BF16),
        in_specs=[vmem, hbm, hbm, hbm],
        out_specs=pl.BlockSpec(memory_space=pl.ANY),
        scratch_shapes=[scratch],
        compiler_params=pltpu.CompilerParams(
            collective_id=0, has_side_effects=True, vmem_limit_bytes=60 * 1024 * 1024
        ),
    )(owner, gradients[0], left_stats, right_stats)


def solution(mesh):
    placed = (
        P("rep", "fsdp", None, None),
        P(),
        P(("fsdp", "rep"), None, None),
        P(("fsdp", "rep"), None, None),
    )
    return jax.shard_map(
        per_device, mesh=mesh, in_specs=placed, out_specs=P("fsdp", None, None), check_vma=False
    )
```

```python
import functools

import jax
import jax.numpy as jnp
from jax import lax
from jax.experimental import pallas as pl
from jax.experimental.pallas import tpu as pltpu
from jax.sharding import PartitionSpec as P

MESH = pl.DeviceIdType.MESH
CORES = 2
PER_Z = 8
LANES = 128
MOVES = (
    (2, 2), (1, 2), (3, 2), (2, 1), (2, 3), (1, 1), (3, 3), (1, 3),
    (3, 1), (2, 0), (0, 2), (1, 0), (3, 0), (0, 1), (0, 3), (0, 0),
)

F32 = jnp.float32
BF16 = jnp.bfloat16


def mm(lhs, rhs):
    return lax.dot_general(lhs, rhs, (((1,), (0,)), ((), ())), preferred_element_type=F32)


def mm_nt(lhs, rhs):
    return lax.dot_general(lhs, rhs, (((1,), (1,)), ((), ())), preferred_element_type=F32)


def mm_tn(lhs, rhs):
    return lax.dot_general(lhs, rhs, (((0,), (0,)), ((), ())), preferred_element_type=F32)


def one_hot(mask):
    return jnp.where(mask, 1.0, 0.0).astype(BF16)


def iota(shape, dim):
    return lax.broadcasted_iota(jnp.int32, shape, dim)


def newton_root(acc):
    factor = 2.5 / jnp.sqrt(jnp.sum(acc * acc))
    m = acc * factor
    mb = m.astype(BF16)
    q = mm(mb, mb) * 0.0625 - 0.625 * m
    t = 1.5625 * m + mm(q.astype(BF16), mb)
    r = 1.25 * q - 0.25 * t
    rest = -0.3125 * m - 0.25 * (1.953125 * t + mm(r.astype(BF16), t.astype(BF16)))
    return factor, rest


def wait_bytes(ref, sem):
    pltpu.make_async_copy(ref, ref, sem).wait()


def kernel(dims, owner, grads, left, right, out, s):
    zs, reps, extent, rb, jb, groups, lanes = dims
    xs = PER_Z // CORES
    plane = PER_Z * reps
    nb = rb * jb
    keys = zs * plane

    f = lax.axis_index("fsdp")
    y = lax.axis_index("rep")
    z = f // PER_Z
    q = lax.rem(f, PER_Z)
    x, c = q // CORES, lax.rem(q, CORES)
    p = q * reps + y

    barrier = pltpu.get_barrier_semaphore()

    def greet_z(k, carry):
        to = (lax.rem(z + k, zs) * PER_Z + q, y)
        pl.semaphore_signal(barrier, inc=1, device_id=to, device_id_type=MESH)
        return carry

    def greet_p(k, carry):
        other = lax.rem(p + k, plane)
        to = (z * PER_Z + other // reps, lax.rem(other, reps))
        pl.semaphore_signal(barrier, inc=1, device_id=to, device_id_type=MESH)
        return carry

    rows_copy = pltpu.make_async_copy(grads, s["rows"], s["local_sem"].at[0])
    rows_copy.start()
    lax.fori_loop(1, zs, greet_z, 0)
    lax.fori_loop(1, plane, greet_p, 0)
    left_copy = pltpu.make_async_copy(left.at[0], s["stats"].at[0], s["local_sem"].at[1])
    left_copy.start()
    right_copy = pltpu.make_async_copy(right.at[0], s["stats"].at[1], s["local_sem"].at[2])
    right_copy.start()

    near = zs // 2

    def rank(away):
        return jnp.where(away < near, zs - 1 - 2 * away, 2 * (away - near))

    def number(at):
        j = sum(jnp.where(at >= rb * t, 1, 0) for t in range(1, jb))
        return (at - j * rb) * jb + j

    p_bits = plane.bit_length() - 1
    n_bits = near.bit_length() - 1
    part = plane * near
    few = near // 2
    sizes = (near, few, few)

    def place(key):
        r = rank(((key >> p_bits) - z) & (zs - 1))
        return (r >> n_bits) * part + ((key & (plane - 1)) << n_bits) + (r & (near - 1))

    blocks = (nb, nb)
    b0, b1 = iota(blocks, 0), iota(blocks, 1)
    owner_r = owner[...].reshape(1, nb)
    owner_c = jnp.sum(jnp.where(b0 == b1, owner_r, 0).astype(F32), axis=1, keepdims=True).astype(jnp.int32)
    same = owner_c == owner_r
    slot_r = jnp.sum(jnp.where(same & (b0 < b1), 1.0, 0.0), axis=0, keepdims=True).astype(jnp.int32)
    key_r = owner_r * reps + slot_r
    swap = one_hot(b0 == number(b1))

    def pick(r, at, use):
        away = near - ((r + 1) >> 1)
        away = jnp.where((r & 1) == 1, away, zs - away)
        wanted = ((z + away) & (zs - 1)) * plane + at
        return mm(one_hot((wanted == key_r) & use), swap).astype(BF16)

    at_far = iota((part, 1), 0)
    s["to_far"][...] = pick(at_far & (near - 1), at_far >> n_bits, at_far >= 0)

    def fill_near():
        for quarter in range(2):
            r = near + quarter * few + (at_far & (few - 1))
            first = (at_far & (near - 1)) < few
            s["to_near"][quarter, 0] = pick(r, at_far >> n_bits, first)
            s["to_near"][quarter, 1] = pick(r, at_far >> n_bits, jnp.logical_not(first))

    def gather(h, k):
        rows = []
        for a in range(reps):
            parts = [s["rows"][a, :, j * extent + h * lanes : j * extent + (h + 1) * lanes] for j in range(jb)]
            rows.append(jnp.concatenate(parts, axis=0))
        if k == 0:
            picked = [mm(s["to_far"][...], row) for row in rows]
        else:
            one, two = s["to_near"][k - 1, 0], s["to_near"][k - 1, 1]
            picked = [mm(one, rows[a]) + mm(two, rows[a + 1]) for a in range(0, reps, 2)]
        picked = [rows.reshape(plane, near, lanes) for rows in picked]
        s["ysend"][k][h] = jnp.concatenate(picked, axis=1).astype(BF16)

    def plane_sends(source, dest, stage, sem):
        def send(core, move):
            qx = lax.rem(x + move[0], xs) * CORES + lax.rem(c + core, CORES)
            py = lax.rem(y + move[1], reps)
            pltpu.make_async_remote_copy(
                src_ref=source(qx, py),
                dst_ref=dest.at[p],
                send_sem=s["send_sem"].at[stage],
                recv_sem=sem,
                device_id=(z * PER_Z + qx, py),
                device_id_type=MESH,
            ).start()

        def step(core, carry):
            for move in MOVES:
                if move != (0, 0):
                    send(core, move)
                else:
                    pl.when(core > 0)(functools.partial(send, core, move))
            return carry

        lax.fori_loop(0, CORES, step, 0)

    def z_send(source, dest, stage, sem, other):
        pltpu.make_async_remote_copy(
            src_ref=source,
            dst_ref=dest,
            send_sem=s["send_sem"].at[stage],
            recv_sem=sem,
            device_id=(other * PER_Z + q, y),
            device_id_type=MESH,
        ).start()

    others_z = pl.ds(0, zs - 1)
    others_p = pl.ds(0, plane - 1)

    def to_place(h, k):
        send, recv = s["ysend"][k], s["yrecv"][k]
        plane_sends(lambda qx, py: send.at[h, qx * reps + py], recv.at[h], 0, s["y_sem"].at[h, k])
        recv[h, p] = send[h, p]

    def to_owner(h, k):
        recv, send, size = s["yrecv"][k], s["zsend"][k], sizes[k]
        wait_bytes(recv.at[h, others_p], s["y_sem"].at[h, k])
        parts = []
        for at in range(PER_Z):
            total = recv[h, at * reps].astype(F32)
            for other in range(1, reps):
                total = total + recv[h, at * reps + other].astype(F32)
            parts.append((total * (1.0 / reps)).astype(BF16))
        averaged = jnp.concatenate(parts, axis=0)
        turn = s["to_z"][...] if k == 0 else s["to_z_few"][...]
        send[h] = mm(turn, averaged).astype(BF16).reshape(size, plane, lanes)

        def step(at, carry):
            r = sum(sizes[:k]) + at
            odd = lax.rem(r, 2)
            away = near - (r + 1) // 2
            other = lax.rem(z + odd * away + (1 - odd) * (zs - away), zs)
            z_send(send.at[h, at], s["zrecv"].at[h, z], 1, s["recv_sem"].at[1, h, 0], other)
            return carry

        lax.fori_loop(0, size - (k == 2), step, 0)
        if k == 2:
            s["zrecv"][h, z] = send[h, size - 1]

    rows_copy.wait()
    gather(0, 0)
    pl.semaphore_wait(barrier, zs - 1 + plane - 1)
    to_place(0, 0)
    row, col = iota((part, part), 0), iota((part, part), 1)
    s["to_z"][...] = one_hot(col == ((row & (plane - 1)) << n_bits) + (row >> p_bits))
    row_few, col_few = iota((part // 2, part // 2), 0), iota((part // 2, part // 2), 1)
    s["to_z_few"][...] = one_hot(col_few == ((row_few & (plane - 1)) << (n_bits - 1)) + (row_few >> p_bits))
    for h in range(1, groups):
        gather(h, 0)
        to_place(h, 0)
    fill_near()
    for h in range(groups):
        gather(h, 1)
        to_owner(h, 0)
        to_place(h, 1)
    for h in range(groups):
        gather(h, 2)
        to_place(h, 2)
    for k in (1, 2):
        for h in range(groups):
            to_owner(h, k)

    slot_c = jnp.sum(jnp.where(same & (b1 < b0), 1.0, 0.0), axis=1, keepdims=True).astype(jnp.int32)
    of_key = one_hot(iota((nb, keys), 1) == place(owner_c * reps + slot_c))
    s["to_block"][...] = mm(one_hot(b1 == number(b0)), of_key).astype(BF16)
    s["to_place"][...] = one_hot(col == ((row & (near - 1)) << p_bits) + (row >> n_bits))

    left_copy.wait()
    right_copy.wait()
    for h in range(groups):
        wait_bytes(s["zrecv"].at[h, others_z], s["recv_sem"].at[1, h, 0])
        s["gmat"][:, h * lanes : (h + 1) * lanes] = s["zrecv"][h].reshape(keys, lanes)
    g = s["gmat"][...]
    dense = g.astype(F32)
    left_factor, left_rest = newton_root(s["stats"][0] + mm_nt(g, g))
    right_factor, right_rest = newton_root(s["stats"][1] + mm_tn(g, g))
    half = 1.5625 * dense + mm(left_rest.astype(BF16), g)
    shaped = 1.5625 * half + mm(half.astype(BF16), right_rest.astype(BF16))
    root_scale = jnp.sqrt(jnp.sqrt(left_factor)) * jnp.sqrt(jnp.sqrt(right_factor))
    mean = 1.0 / (extent * extent)
    grad_rms = jnp.sqrt(jnp.sum(dense * dense) * mean)
    shaped_rms = jnp.sqrt(jnp.sum(shaped * shaped) * mean * (root_scale * root_scale) + 1e-06)
    update = (shaped * (root_scale * (grad_rms / shaped_rms))).astype(BF16)
    for h in range(groups):
        s["bsend"][h] = update[:, h * lanes : (h + 1) * lanes].reshape(zs, plane, lanes)

    def back_z(h, half):
        def send(other, r):
            z_send(s["bsend"].at[h, other], s["brecv"].at[h, half, r], 2, s["recv_sem"].at[2, h, half], other)

        def near_step(k, carry):
            r = zs - 2 - k
            odd = lax.rem(r, 2)
            away = near - (r + 1) // 2
            send(lax.rem(z + odd * (zs - away) + (1 - odd) * away, zs), r - near)
            return carry

        def far_step(k, carry):
            other = lax.rem(k, 2) * near + k // 2
            r = rank(lax.rem(z - other + zs, zs))
            pl.when(r < near)(functools.partial(send, other, r))
            return carry

        if half == 1:
            lax.fori_loop(0, near - 1, near_step, 0)
            s["brecv"][h, 1, near - 1] = s["bsend"][h, z]
        else:
            lax.fori_loop(0, zs, far_step, 0)

    for half in (1, 0):
        for h in range(groups):
            back_z(h, half)

    def back(h, half):
        wait_bytes(s["brecv"].at[h, half, pl.ds(0, near - half)], s["recv_sem"].at[2, h, half])
        rows = mm(s["to_place"][...], s["brecv"][h, half].reshape(part, lanes)).astype(BF16)
        s["psend"][h, half] = rows.reshape(PER_Z, reps * near, lanes)
        plane_sends(lambda qx, py: s["psend"].at[h, half, qx], s["precv"].at[h, half], 3, s["recv_sem"].at[3, h, half])
        s["precv"][h, half, p] = s["psend"][h, half, q]

    def near_rows(h):
        wait_bytes(s["precv"].at[h, 1, others_p], s["recv_sem"].at[3, h, 1])
        piece = s["precv"][h, 1].astype(F32)
        for a in range(reps):
            at_a = piece[:, a * near : (a + 1) * near].reshape(part, lanes).astype(BF16)
            s["near"][h, a] = mm(s["to_block"][:, part:], at_a).astype(BF16)

    def write(h):
        wait_bytes(s["precv"].at[h, 0, others_p], s["recv_sem"].at[3, h, 0])
        piece = s["precv"][h, 0].astype(F32)
        for a in range(reps):
            at_a = piece[:, a * near : (a + 1) * near].reshape(part, lanes).astype(BF16)
            rows = mm(s["to_block"][:, :part], at_a).astype(BF16) + s["near"][h, a]
            for j in range(jb):
                at = j * extent + h * lanes
                s["rows"][a, :, at : at + lanes] = rows[j * rb : (j + 1) * rb]
        for j in range(jb):
            at = pl.ds(j * extent + h * lanes, lanes)
            pltpu.make_async_copy(s["rows"].at[:, :, at], out.at[:, :, at], s["local_sem"].at[3]).start()

    for h in range(groups):
        back(h, 1)
    for h in range(groups):
        back(h, 0)
        near_rows(h)
        if h > 0:
            write(h - 1)
    write(groups - 1)

    wait_bytes(s["rows"], s["local_sem"].at[3])
    wait_bytes(s["precv"].at[:, :, others_p], s["send_sem"].at[0])
    wait_bytes(s["zrecv"].at[:, others_z], s["send_sem"].at[1])
    wait_bytes(s["bsend"].at[:, others_z], s["send_sem"].at[2])
    wait_bytes(s["precv"].at[:, :, others_p], s["send_sem"].at[3])


def per_device(gradients, owner, left_stats, right_stats):
    reps = lax.axis_size("rep")
    owners = lax.axis_size("fsdp")
    rows, rb, width = gradients.shape[1:]
    extent = rows * owners
    jb = width // extent
    nb = rb * jb
    zs = owners // PER_Z
    plane = PER_Z * reps
    groups = extent // LANES
    keys = owners * reps
    assert rows == reps and keys == extent

    vmem = pl.BlockSpec(memory_space=pltpu.VMEM)
    hbm = pl.BlockSpec(memory_space=pltpu.HBM)
    dma = pltpu.SemaphoreType.DMA
    by_z = pltpu.VMEM((groups, zs, plane, LANES), BF16)
    by_half = pltpu.VMEM((groups, 2, zs // 2, plane, LANES), BF16)
    by_place = pltpu.VMEM((groups, 2, plane, rows * zs // 2, LANES), BF16)
    sizes = (zs // 2, zs // 4, zs // 4)
    by_part = [pltpu.VMEM((groups, plane, rows * size, LANES), BF16) for size in sizes]
    scratch = dict(
        rows=pltpu.VMEM((rows, rb, width), BF16),
        stats=pltpu.VMEM((2, extent, extent), F32),
        ysend=by_part,
        yrecv=by_part,
        zsend=[pltpu.VMEM((groups, size, plane, LANES), BF16) for size in sizes],
        zrecv=by_z,
        bsend=by_z,
        brecv=by_half,
        psend=pltpu.VMEM((groups, 2, PER_Z, rows * zs // 2, LANES), BF16),
        precv=by_place,
        near=pltpu.VMEM((groups, rows, nb, LANES), BF16),
        to_far=pltpu.VMEM((keys // 2, nb), BF16),
        to_near=pltpu.VMEM((2, 2, keys // 2, nb), BF16),
        to_z_few=pltpu.VMEM((keys // 4, keys // 4), BF16),
        to_block=pltpu.VMEM((nb, keys), BF16),
        to_place=pltpu.VMEM((keys // 2, keys // 2), BF16),
        to_z=pltpu.VMEM((keys // 2, keys // 2), BF16),
        gmat=pltpu.VMEM((extent, extent), BF16),
        local_sem=dma((4,)),
        y_sem=dma((groups, 3)),
        send_sem=dma((4,)),
        recv_sem=dma((4, groups, 2)),
    )
    return pl.pallas_call(
        functools.partial(kernel, (zs, reps, extent, rb, jb, groups, LANES)),
        out_shape=jax.ShapeDtypeStruct((rows, rb, width), BF16),
        in_specs=[vmem, hbm, hbm, hbm],
        out_specs=pl.BlockSpec(memory_space=pl.ANY),
        scratch_shapes=[scratch],
        compiler_params=pltpu.CompilerParams(
            collective_id=0, has_side_effects=True, vmem_limit_bytes=60 * 1024 * 1024
        ),
    )(owner, gradients[0], left_stats, right_stats)


def solution(mesh):
    placed = (
        P("rep", "fsdp", None, None),
        P(),
        P(("fsdp", "rep"), None, None),
        P(("fsdp", "rep"), None, None),
    )
    return jax.shard_map(
        per_device, mesh=mesh, in_specs=placed, out_specs=P("fsdp", None, None), check_vma=False
    )
```
